128 devices in a mesh: row: 16 (over y, x), col: 8 (over z, core).
Axes of the slice: x: 4, y: 4, z: 4, core: 2. Of those that a mesh axis runs over, the one named last changes fastest.
Arguments:
- s_panel: float32 [16384, 512], P('row', 'col'), may hold values from -1.5 to 1.5
- l_inv: float32 [512, 512], P(None, 'col'), may hold values from -1 to 8, as said below
- h_diag: float32 [512, 512], P(None, 'col'), may hold values from -0.25 to 0.25
- h_panel: float32 [16384, 512], P('row', 'col'), may hold values from -1.5 to 1.5
- h_trail: float32 [16384, 16384], P('row', 'col'), may hold values from -6 to 6
Outputs:
- l_panel: float32 [16384, 512], P('row', 'col')
- h_panel_out: float32 [16384, 512], P('row', 'col')
- h_trail_out: float32 [16384, 16384], P('row', 'col')
The draws below stay inside these ranges and needn't reach their ends.
Inputs may be any that keep to these rules, and one draw needn't show every extreme that they name: l_inv is lower triangular with a positive diagonal.
All inputs are finite; a program needn't handle non-finite values.
Results may differ from the reference program's by a relative error of at most 0.00021.
Values sent between devices are 32-bit elements; how exact they have to be, the bound alone decides.
A program may use at most 128 MiB of HBM per device.

```python
import math
import jax
import jax.numpy as jnp
from jax import lax

NB = 512
M = 16384


def draw_l_inv(key, part):
    key = jax.random.fold_in(key, 7)
    diag_key, off_key = jax.random.split(key, 2)
    row_index = jnp.arange(NB)[:, None]
    col_index = jnp.arange(NB)[None, :]
    diagonal = jnp.exp(jax.random.uniform(diag_key, (NB,), jnp.float32, math.log(0.5), math.log(2.0)))
    offdiag = jax.random.truncated_normal(off_key, -3.0, 3.0, (NB, NB), jnp.float32) * (0.6 / math.sqrt(NB))
    strict = jnp.where(col_index < row_index, offdiag, 0.0)
    whole = strict + jnp.where(row_index == col_index, diagonal[:, None], 0.0)
    return whole.astype(jnp.float32)


def steps_of(rng, dims, cuts, low, top_value):
    def one(position, blocks):
        steps = jax.random.uniform(jax.random.fold_in(jax.random.fold_in(rng, 6), position), (blocks,), jnp.float32, low / len(cuts), top_value / len(cuts))
        return jnp.repeat(jnp.exp(steps), dims[position] // blocks).reshape((-1,) + (1,) * (len(dims) - position - 1))

    gain = one(*cuts[0])
    for cut in cuts[1:]:
        gain = gain * one(*cut)
    return gain


def normal_values(rng, dims, scale, limit, cuts=(), kind=jnp.bfloat16):
    entries = scale * jax.random.normal(rng, dims, jnp.float32)
    if cuts:
        entries = entries * steps_of(rng, dims, cuts, -0.22, 0.18)
    return jnp.clip(entries, -limit, limit).astype(kind)


def setup_inputs(seed: int = 0) -> dict:
    arg_keys = jax.random.split(jax.random.key(seed), 6)
    s_panel = normal_values(arg_keys[0], (M, NB), 0.25, 1.5, ((0, 16), (1, 8)), jnp.float32)
    l_inv = draw_l_inv(jax.random.fold_in(arg_keys[5], 71), 0)
    h_diag = normal_values(arg_keys[2], (NB, NB), NB ** -0.5, 0.25, ((1, 8),), jnp.float32)
    h_panel = normal_values(arg_keys[3], (M, NB), 0.25, 1.5, ((0, 16), (1, 8)), jnp.float32)
    h_trail = normal_values(arg_keys[4], (M, M), 1.0, 6.0, ((0, 16), (1, 8)), jnp.float32)
    return dict(s_panel=s_panel, l_inv=l_inv, h_diag=h_diag, h_panel=h_panel, h_trail=h_trail)


def product(first, second):
    return jnp.dot(first, second, precision=lax.Precision.HIGHEST, preferred_element_type=jnp.float32)


def reference(s_panel, l_inv, h_diag, h_panel, h_trail):
    l_panel = product(s_panel, l_inv.T)
    diag_half = product(l_inv, h_diag)
    diag_new = product(diag_half, l_inv.T)
    coupled = product(h_panel, l_inv.T)
    h_panel_out = coupled - product(l_panel, diag_new)
    left_side = jnp.concatenate([l_panel, h_panel_out], axis=1)
    right_side = jnp.concatenate([coupled, l_panel], axis=1)
    h_trail_out = h_trail - product(left_side, right_side.T)
    return l_panel, h_panel_out, h_trail_out
```

```python
import functools

import jax
import jax.numpy as jnp
from jax import lax
from jax.experimental import pallas as pl
from jax.experimental.pallas import tpu as pltpu
from jax.sharding import PartitionSpec as P

MESH = pl.DeviceIdType.MESH
F32, BF16 = jnp.float32, jnp.bfloat16
ROWS, NB, SIDE = 1024, 512, 64
UNIT = 64
NW = ROWS // UNIT
UNITS = 64
HOP = 5
LEAD = 4
GAP = 3
LAST = UNITS + LEAD + GAP + 4 * HOP
W_STEP = 12
W_FAR, W_DONE = W_STEP + 5, W_STEP + 8
Q_STEP = W_DONE
U_STEP = 55
U_READY = LAST - 42


def split(value):
    high = value.astype(BF16)
    return high, (value - high.astype(F32)).astype(BF16)


def dot3(a_high, a_low, b_high, b_low, b_dim):
    dims = (((1,), (b_dim,)), ((), ()))
    one = lambda a, b: lax.dot_general(a, b, dims, preferred_element_type=F32)
    return one(a_high, b_high) + (one(a_high, b_low) + one(a_low, b_high))


def half_turn(tile):
    return pltpu.roll(tile, SIDE, 1)


def kernel(s_ref, x_ref, d_ref, p_ref, t_hbm, low_ref, red_ref, out_hbm,
           w_all, xh_all, items, trail, left_high, left_low, q_high, q_low,
           x_high, x_low, xt_high, xt_low, m_high, m_low, n_high, n_low,
           d_full, z_high, z_low, a_high, a_low, b_high, b_low,
           own_recv, z_recv, far_recv, sib_recv, item_recv,
           xz_recv, xf_recv, xs_recv, own_send, sib_send, x_send, item_send,
           load_sem, store_sem):
    r, j = lax.axis_index("row"), lax.axis_index("col")
    y, x, z, c = r // 4, r % 4, j // 2, j % 2
    z_up, z_down, z_far = ((z + 1) % 4) * 2 + c, ((z + 3) % 4) * 2 + c, ((z + 2) % 4) * 2 + c
    j_sib = z * 2 + 1 - c
    up, down, sib = (r, z_up), (r, z_down), (r, j_sib)
    plane = [
        (y * 4 + (x + 1) % 4, j), (y * 4 + (x + 3) % 4, j),
        (((y + 1) % 4) * 4 + x, j), (((y + 3) % 4) * 4 + x, j),
    ]
    barrier = pltpu.get_barrier_semaphore()
    for device in plane + [up, down, sib]:
        pl.semaphore_signal(barrier, inc=1, device_id=device, device_id_type=MESH)

    load = pltpu.make_async_copy(t_hbm, trail, load_sem)
    load.start()
    lanes = lambda k: pl.ds(pl.multiple_of(k * 128, 128), 128)
    lane = lambda rows, width=128: lax.broadcasted_iota(jnp.int32, (rows, width), 1)
    xh_all[:, lanes(j)] = jnp.concatenate([x_ref[...], d_ref[...]], axis=1)
    w_all[:, lanes(j)] = jnp.concatenate([s_ref[...], p_ref[...]], axis=1)
    pl.semaphore_wait(barrier, 7)

    def send(ref, send_sem, recv_sem, device):
        return pltpu.make_async_remote_copy(
            src_ref=ref, dst_ref=ref, send_sem=send_sem, recv_sem=recv_sem,
            device_id=device, device_id_type=MESH)

    def arrived(ref, sem):
        send(ref, sib_send.at[0], sem, sib).wait_recv()

    def rows_of(w):
        return pl.ds(pl.multiple_of(w * UNIT, UNIT), UNIT)

    def chunk(w, k):
        return w_all.at[rows_of(w), lanes(k)]

    f = (y + 4 - z) % 4
    outs, depth = [], []
    for m in range(2):
        e = (x + 4 - (2 * c + m)) % 4
        at = lambda a, b, e=e: (e == a) & (f == b)
        to_x = at(0, 0) | at(1, 1) | at(3, 3) | at(1, 2)
        to_up = at(1, 0) | at(1, 1) | at(1, 2)
        to_down = at(3, 0) | at(3, 3) | at(3, 2) | at(2, 1)
        outs.append([to_x, to_x, to_up, to_down])
        third = at(0, 3) | at(2, 3) | at(0, 1) | at(3, 2) | at(2, 1) | at(1, 2)
        depth.append(jnp.where(at(0, 0), 0, jnp.where(
            at(1, 0) | at(3, 0), 1, jnp.where(at(1, 1) | at(3, 3), 2, jnp.where(third, 3, 4)))))

    def unit(q):
        late = q >= 16
        block = jnp.where(late, (q + 32) // 3 - 16, q)
        which = (q + 32) % 3
        slot = jnp.where(late, jnp.where(which == 0, z + 3, jnp.where(which == 1, z + 1, z + 2)), z) % 4
        return rows_of(block), pl.ds(pl.multiple_of(slot * 256, 256), 256)

    def unit_at(t):
        early = t < LEAD + 16
        late = t >= LEAD + 16 + GAP
        return jnp.where(late, t - LEAD - GAP, t - LEAD), (t >= LEAD) & (early | (late & (t < LEAD + GAP + UNITS)))

    own_x = xh_all.at[:, lanes(j)]
    send(own_x, sib_send.at[2], xs_recv, sib).start()
    send(own_x, x_send.at[0], xz_recv.at[0], up).start()
    send(own_x, x_send.at[1], xz_recv.at[1], down).start()

    def prepare():
        for p in range(4):
            at_p, first, second = pl.ds(p * 128, 128), xh_all[:, 256 * p:256 * p + 128], xh_all[:, 256 * p + 128:256 * p + 256]
            lower = lane(NB) < SIDE
            xv = jnp.where(lower, first, half_turn(second))
            dv = jnp.where(lower, half_turn(first), second)
            x_high[:, at_p], x_low[:, at_p] = split(xv)
            m_high[:, at_p], m_low[:, at_p] = split(dv)
            xt_high[at_p, :], xt_low[at_p, :] = split(jnp.transpose(xv))
            z_first = jnp.where(lower, 0.0, half_turn(xv))
            z_second = jnp.where(lower, 0.0, xv)
            z_high[:, 256 * p:256 * p + 128], z_low[:, 256 * p:256 * p + 128] = split(z_first)
            z_high[:, 256 * p + 128:256 * p + 256], z_low[:, 256 * p + 128:256 * p + 256] = split(z_second)

    def half_product():
        value = dot3(x_high[...], x_low[...], m_high[...], m_low[...], 0)
        n_high[...], n_low[...] = split(value)

    def diag_product():
        value = dot3(n_high[...], n_low[...], xt_high[...], xt_low[...], 0)
        d_full[...] = value
        m_high[...], m_low[...] = split(value)

    def inner_product():
        value = dot3(m_high[...], m_low[...], x_high[...], x_low[...], 0)
        lower = lane(NB) < SIDE
        for p in range(4):
            tile = value[:, 128 * p:128 * p + 128]
            for h in range(2):
                at_h = pl.ds(256 * p + 128 * h, 128)
                part = jnp.where(lower, -(tile if h == 0 else half_turn(tile)), 0.0)
                high, low = split(part)
                z_high[:, at_h] = jnp.where(lower, high, z_high[:, at_h])
                z_low[:, at_h] = jnp.where(lower, low, z_low[:, at_h])
        mine = d_full[:, pl.ds(pl.multiple_of(z * 128, 128), 128)]
        mine = jnp.where(c == 0, half_turn(mine), mine)
        row_id = lax.broadcasted_iota(jnp.int32, (NB, 128), 0)
        pick = jnp.where(row_id == lane(NB) + SIDE * j, 1.0, 0.0)
        z_high[:, 1024:1152], z_low[:, 1024:1152] = split(jnp.where(lower, pick, -mine))

    def weights(n, wide):
        at_n = pl.ds(1024, 128) if not wide else pl.ds(pl.multiple_of(n * 256, 256), 256)
        value = dot3(xt_high[...], xt_low[...], z_high[:, at_n], z_low[:, at_n], 0)
        lower = lane(NB) < SIDE
        if wide:
            turned = jnp.concatenate(
                [jnp.where(lower, half_turn(value[:, h * 128:h * 128 + 128]), 0.0) for h in range(2)], axis=1)
        else:
            turned = jnp.where(lower, 0.0, half_turn(value))
        for part, shift in ((value, 0), (turned, SIDE)):
            high, low = split(part)
            for k in range(8):
                q_high[k * 128 + shift:k * 128 + shift + SIDE, at_n] = high[k * SIDE:(k + 1) * SIDE]
                q_low[k * 128 + shift:k * 128 + shift + SIDE, at_n] = low[k * SIDE:(k + 1) * SIDE]

    def left_task(g, n):
        rows = pl.ds(pl.multiple_of(g * 256, 256), 256)

        @pl.when(n == 0)
        def _():
            a_high[...], a_low[...] = split(w_all[rows, :])

        @pl.when(n < 4)
        def _():
            at_n = pl.ds(pl.multiple_of(n * 256, 256), 256)
            value = dot3(a_high[...], a_low[...], q_high[:, at_n], q_low[:, at_n], 0)
            left_high[rows, at_n], left_low[rows, at_n] = split(value)

        @pl.when(n == 4)
        def _():
            value = dot3(a_high[...], a_low[...], q_high[:, 1024:1152], q_low[:, 1024:1152], 0)
            low_ref[rows, :] = value[:, :SIDE]
            red_ref[rows, :] = half_turn(value)[:, :SIDE]

    def store(block, m):
        cols = pl.ds(pl.multiple_of(m * ROWS + block * 128, 128), 128)
        return pltpu.make_async_copy(trail.at[:, cols], out_hbm.at[:, cols], store_sem)

    def trail_task(block, i):
        @pl.when(i == 0)
        def _():
            for m in range(2):
                value = items[m, pl.ds(pl.multiple_of(block * 128, 128), 128), :]
                b_high[m * 128:m * 128 + 128, :], b_low[m * 128:m * 128 + 128, :] = split(value)

        rows = pl.ds(pl.multiple_of(i * 256, 256), 256)
        value = dot3(left_high[rows, :], left_low[rows, :], b_high[...], b_low[...], 1)
        for m in range(2):
            cols = pl.ds(pl.multiple_of(m * ROWS + block * 128, 128), 128)
            trail[rows, cols] = trail[rows, cols] - value[:, m * 128:m * 128 + 128]

        @pl.when(i == 3)
        def _():
            for m in range(2):
                store(block, m).start()

    def step(t, carry):
        @pl.when(t < 8)
        def _():
            for i in range(2):
                w = t * 2 + i
                send(chunk(w, j), sib_send.at[0], own_recv.at[w], sib).start()
                send(chunk(w, j), own_send.at[0], z_recv.at[0, w], up).start()
                send(chunk(w, j), own_send.at[1], z_recv.at[1, w], down).start()

        @pl.when((t >= 2) & (t < 2 + NW))
        def _():
            arrived(chunk(t - 2, j_sib), own_recv.at[t - 2])

        for m in range(2):
            q_copy, ready = unit_at(t + 2)

            @pl.when((depth[m] == 0) & ready)
            def _():
                at = unit(q_copy)
                pltpu.make_async_copy(w_all.at[at[0], at[1]], items.at[m, at[0], at[1]], item_recv.at[m, q_copy]).start()

            q, here = unit_at(t - HOP * depth[m])

            @pl.when(here)
            def _():
                at = unit(q)
                part = items.at[m, at[0], at[1]]
                arrived(part, item_recv.at[m, q])
                for d in range(4):
                    @pl.when(outs[m][d])
                    def _():
                        send(part, item_send.at[m, d], item_recv.at[m, q], plane[d]).start()

        @pl.when((t >= W_STEP) & (t < W_STEP + 2 * NW) & ((t - W_STEP) % 2 == 0))
        def _():
            w = (t - W_STEP) // 2
            arrived(chunk(w, z_down), z_recv.at[0, w])
            arrived(chunk(w, z_up), z_recv.at[1, w])

            @pl.when(c == 0)
            def _():
                send(chunk(w, z_down), own_send.at[2], far_recv.at[w], up).start()

            @pl.when(c == 1)
            def _():
                send(chunk(w, z_up), own_send.at[2], far_recv.at[w], down).start()

            send(chunk(w, z_down), sib_send.at[1], sib_recv.at[w], sib).start()
            send(chunk(w, z_up), sib_send.at[1], sib_recv.at[w], sib).start()

        @pl.when((t >= W_FAR) & (t < W_FAR + 2 * NW) & ((t - W_FAR) % 2 == 0))
        def _():
            w = (t - W_FAR) // 2
            arrived(chunk(w, z_far), far_recv.at[w])
            send(chunk(w, z_far), sib_send.at[1], sib_recv.at[w], sib).start()

        @pl.when((t >= W_DONE) & (t < W_DONE + 2 * NW) & ((t - W_DONE) % 2 == 0))
        def _():
            w = (t - W_DONE) // 2
            arrived(w_all.at[rows_of(w), pl.ds(0, 384)], sib_recv.at[w])

        @pl.when(t == W_STEP - 1)
        def _():
            first, second = xh_all.at[:, lanes(z_down)], xh_all.at[:, lanes(z_up)]
            arrived(first, xz_recv.at[0])
            arrived(second, xz_recv.at[1])

            @pl.when(c == 0)
            def _():
                send(first, x_send.at[2], xf_recv, up).start()

            @pl.when(c == 1)
            def _():
                send(second, x_send.at[2], xf_recv, down).start()

            send(first, sib_send.at[2], xs_recv, sib).start()
            send(second, sib_send.at[2], xs_recv, sib).start()

        @pl.when(t == W_FAR - 1)
        def _():
            far = xh_all.at[:, lanes(z_far)]
            arrived(far, xf_recv)
            send(far, sib_send.at[2], xs_recv, sib).start()

        @pl.when(t == Q_STEP)
        def _():
            arrived(xh_all.at[:, pl.ds(0, 512)], xs_recv)
            prepare()

        pl.when(t == Q_STEP + 1)(half_product)
        pl.when(t == Q_STEP + 2)(diag_product)
        pl.when(t == Q_STEP + 3)(inner_product)

        @pl.when((t >= Q_STEP + 4) & (t < Q_STEP + 8))
        def _():
            weights(t - Q_STEP - 4, True)

        pl.when(t == Q_STEP + 8)(lambda: weights(0, False))

        for g in range(4):
            start = max(Q_STEP + 9, W_DONE + 6 + 8 * g)

            @pl.when((t >= start) & (t < start + 5))
            def _():
                left_task(g, t - start)

        @pl.when(t == U_STEP - 1)
        def _():
            pltpu.make_async_copy(t_hbm, trail, load_sem).wait()

        dense = t < U_STEP + 16
        block = jnp.where(dense, (t - U_STEP) // 4, (t - U_READY) // 6)
        i = jnp.where(dense, (t - U_STEP) % 4, (t - U_READY) % 6)

        @pl.when((t >= U_STEP) & (dense | (block >= 4)) & (i < 4))
        def _():
            trail_task(block, i)

        return carry

    lax.fori_loop(0, LAST, step, 0)
    lax.fori_loop(0, 4, lambda i, carry: (trail_task(7, i), carry)[1], 0)

    own = w_all.at[:, lanes(j)]
    done = lambda ref, sem: send(ref, sem, own_recv.at[0], sib).wait_send()
    for i in range(3):
        done(own, own_send.at[i])
        done(own_x, x_send.at[i])
    done(own, sib_send.at[0])
    done(w_all.at[:, pl.ds(0, 384)], sib_send.at[1])
    done(xh_all.at[:, pl.ds(0, 512)], sib_send.at[2])
    for m in range(2):
        for d in range(4):
            @pl.when(outs[m][d])
            def _():
                done(items.at[m], item_send.at[m, d])
    pltpu.make_async_copy(trail, out_hbm, store_sem).wait()


def on_device(s_panel, l_inv, h_diag, h_panel, h_trail):
    vmem = pl.BlockSpec(memory_space=pltpu.VMEM)
    hbm = pl.BlockSpec(memory_space=pl.ANY)
    dma = pltpu.SemaphoreType.DMA
    mats = [pltpu.VMEM((NB, NB), BF16)] * 8
    return pl.pallas_call(
        kernel,
        out_shape=(
            jax.ShapeDtypeStruct(s_panel.shape, F32),
            jax.ShapeDtypeStruct(h_panel.shape, F32),
            jax.ShapeDtypeStruct(h_trail.shape, F32),
        ),
        in_specs=[vmem, vmem, vmem, vmem, hbm],
        out_specs=(vmem, vmem, hbm),
        scratch_shapes=[
            pltpu.VMEM((ROWS, 1024), F32), pltpu.VMEM((NB, 1024), F32),
            pltpu.VMEM((2, ROWS, 1024), F32), pltpu.VMEM((ROWS, 2 * ROWS), F32),
            pltpu.VMEM((ROWS, 1024), BF16), pltpu.VMEM((ROWS, 1024), BF16),
            pltpu.VMEM((1024, 1152), BF16), pltpu.VMEM((1024, 1152), BF16),
            *mats,
            pltpu.VMEM((NB, NB), F32), pltpu.VMEM((NB, 1152), BF16), pltpu.VMEM((NB, 1152), BF16),
            *[pltpu.VMEM((256, 1024), BF16)] * 4,
            dma((NW,)), dma((2, NW)), dma((NW,)), dma((NW,)), dma((2, UNITS)),
            dma((2,)), dma, dma, dma((3,)), dma((3,)), dma((3,)), dma((2, 4)),
            dma, dma,
        ],
        compiler_params=pltpu.CompilerParams(
            collective_id=0, has_side_effects=True, vmem_limit_bytes=56 * 2**20),
        cost_estimate=pl.CostEstimate(flops=22 * 10**9, bytes_accessed=20 * 2**20, transcendentals=0),
    )(s_panel, l_inv, h_diag, h_panel, h_trail)


def solution(mesh):
    in_specs = (P("row", "col"), P(None, "col"), P(None, "col"), P("row", "col"), P("row", "col"))
    out_specs = (P("row", "col"), P("row", "col"), P("row", "col"))
    return jax.shard_map(
        on_device, mesh=mesh, in_specs=in_specs, out_specs=out_specs, check_vma=False
    )
```

```python
import functools

import jax
import jax.numpy as jnp
from jax import lax
from jax.experimental import pallas as pl
from jax.experimental.pallas import tpu as pltpu
from jax.sharding import PartitionSpec as P

MESH = pl.DeviceIdType.MESH
F32, BF16 = jnp.float32, jnp.bfloat16
ROWS, NB, SIDE = 1024, 512, 64
NW = ROWS // 128
UNITS = 64
HOP = 5
LEAD = 4
GAP = 3
LAST = UNITS + LEAD + GAP + 4 * HOP
W_STEP = 12
W_FAR, W_DONE = W_STEP + 5, W_STEP + 8
W_OPEN = 2
X_STEP, X_FAR = W_STEP - 1, W_STEP + 4
Q_STEP = W_DONE
U_READY = LAST - 42


def split(value):
    high = value.astype(BF16)
    return high, (value - high.astype(F32)).astype(BF16)


def dot3(a_high, a_low, b_high, b_low, b_dim):
    dims = (((1,), (b_dim,)), ((), ()))
    one = lambda a, b: lax.dot_general(a, b, dims, preferred_element_type=F32)
    return one(a_high, b_high) + (one(a_high, b_low) + one(a_low, b_high))


def half_turn(tile):
    return pltpu.roll(tile, SIDE, 1)


def kernel(s_hbm, x_hbm, d_hbm, p_hbm, t_hbm, low_ref, red_ref, trail,
           w_all, xh_all, items, left_high, left_low, q_high, q_low,
           x_high, x_low, xt_high, xt_low, m_high, m_low, n_high, n_low,
           d_full, z_high, z_low, a_high, a_low, b_high, b_low,
           own_recv, z_recv, far_recv, sib_recv, item_recv,
           xz_recv, xf_recv, xs_recv, own_send, sib_send, x_send, item_send,
           fetch_sem, load_sem):
    r, j = lax.axis_index("row"), lax.axis_index("col")
    y, x, z, c = r // 4, r % 4, j // 2, j % 2
    z_up, z_down, z_far = ((z + 1) % 4) * 2 + c, ((z + 3) % 4) * 2 + c, ((z + 2) % 4) * 2 + c
    j_sib = z * 2 + 1 - c
    up, down, sib = (r, z_up), (r, z_down), (r, j_sib)
    plane = [
        (y * 4 + (x + 1) % 4, j), (y * 4 + (x + 3) % 4, j),
        (((y + 1) % 4) * 4 + x, j), (((y + 3) % 4) * 4 + x, j),
    ]
    barrier = pltpu.get_barrier_semaphore()
    for device in plane + [up, down, sib]:
        pl.semaphore_signal(barrier, inc=1, device_id=device, device_id_type=MESH)

    slot = lambda k: pl.ds(pl.multiple_of(k * 128, 128), 128)
    lane = lambda rows, width=128: lax.broadcasted_iota(jnp.int32, (rows, width), 1)
    fetches = []
    for h, (panel, matrix) in enumerate(((s_hbm, x_hbm), (p_hbm, d_hbm))):
        at_h = pl.ds(pl.multiple_of(j * 128 + h * SIDE, SIDE), SIDE)
        fetches.append(pltpu.make_async_copy(matrix, xh_all.at[at_h, :], fetch_sem.at[8, h]))
        for w in range(NW):
            fetches.append(pltpu.make_async_copy(
                panel.at[:, pl.ds(w * 128, 128)], w_all.at[w, at_h, :], fetch_sem.at[w, h]))
    for fetch in fetches:
        fetch.start()
    load = pltpu.make_async_copy(t_hbm, trail, load_sem)
    load.start()
    for fetch in fetches:
        fetch.wait()
    pl.semaphore_wait(barrier, 7)

    def send(ref, send_sem, recv_sem, device):
        return pltpu.make_async_remote_copy(
            src_ref=ref, dst_ref=ref, send_sem=send_sem, recv_sem=recv_sem,
            device_id=device, device_id_type=MESH)

    def arrived(ref, sem):
        send(ref, sib_send.at[0], sem, sib).wait_recv()

    def chunk(w, k):
        return w_all.at[w, slot(k), :]

    f = (y + 4 - z) % 4
    outs, depth = [], []
    for m in range(2):
        e = (x + 4 - (2 * c + m)) % 4
        at = lambda a, b, e=e: (e == a) & (f == b)
        to_x = at(0, 0) | at(1, 1) | at(3, 3) | at(1, 2)
        to_up = at(1, 0) | at(1, 1) | at(1, 2)
        to_down = at(3, 0) | at(3, 3) | at(3, 2) | at(2, 1)
        outs.append([to_x, to_x, to_up, to_down])
        third = at(0, 3) | at(2, 3) | at(0, 1) | at(3, 2) | at(2, 1) | at(1, 2)
        depth.append(jnp.where(at(0, 0), 0, jnp.where(
            at(1, 0) | at(3, 0), 1, jnp.where(at(1, 1) | at(3, 3), 2, jnp.where(third, 3, 4)))))

    def unit(q):
        late = q >= 16
        block = jnp.where(late, (q + 32) // 6 - 8, q // 2)
        which = (q + 32) % 6 // 2
        level = jnp.where(late, jnp.where(which == 0, z + 3, jnp.where(which == 1, z + 1, z + 2)), z) % 4
        return block, slot(level * 2 + q % 2)

    def unit_at(t):
        early = t < LEAD + 16
        late = t >= LEAD + 16 + GAP
        return jnp.where(late, t - LEAD - GAP, t - LEAD), (t >= LEAD) & (early | (late & (t < LEAD + GAP + UNITS)))

    own_x = xh_all.at[slot(j), :]
    send(own_x, sib_send.at[2], xs_recv, sib).start()
    send(own_x, x_send.at[0], xz_recv.at[0], up).start()
    send(own_x, x_send.at[1], xz_recv.at[1], down).start()

    def prepare():
        lower = lane(NB) < SIDE
        for p in range(4):
            rows = pl.ds(p * 128, 128)
            pair = [xh_all[256 * p + 128 * h:256 * p + 128 * h + 128, :] for h in range(2)]
            xt = jnp.concatenate([tile[:SIDE] for tile in pair], axis=0)
            dt = jnp.concatenate([tile[SIDE:] for tile in pair], axis=0)
            xt_high[rows, :], xt_low[rows, :] = split(xt)
            m_high[rows, :], m_low[rows, :] = split(dt)
            xv = jnp.transpose(xt)
            x_high[:, rows], x_low[:, rows] = split(xv)
            first, second = pl.ds(256 * p, 128), pl.ds(256 * p + 128, 128)
            z_high[:, first], z_low[:, first] = split(jnp.where(lower, 0.0, half_turn(xv)))
            z_high[:, second], z_low[:, second] = split(jnp.where(lower, 0.0, xv))

    def half_product():
        value = dot3(x_high[...], x_low[...], m_high[...], m_low[...], 1)
        n_high[...], n_low[...] = split(value)

    def diag_product():
        value = dot3(n_high[...], n_low[...], xt_high[...], xt_low[...], 0)
        d_full[...] = value
        m_high[...], m_low[...] = split(value)

    def inner_product():
        value = dot3(m_high[...], m_low[...], x_high[...], x_low[...], 0)
        lower = lane(NB) < SIDE
        for p in range(4):
            tile = value[:, 128 * p:128 * p + 128]
            for h in range(2):
                at_h = pl.ds(256 * p + 128 * h, 128)
                part = jnp.where(lower, -(tile if h == 0 else half_turn(tile)), 0.0)
                high, low = split(part)
                z_high[:, at_h] = jnp.where(lower, high, z_high[:, at_h])
                z_low[:, at_h] = jnp.where(lower, low, z_low[:, at_h])
        mine = d_full[:, pl.ds(pl.multiple_of(z * 128, 128), 128)]
        mine = jnp.where(c == 0, half_turn(mine), mine)
        row_id = lax.broadcasted_iota(jnp.int32, (NB, 128), 0)
        pick = jnp.where(row_id == lane(NB) + SIDE * j, 1.0, 0.0)
        z_high[:, 1024:1152], z_low[:, 1024:1152] = split(jnp.where(lower, pick, -mine))

    def weights(n, wide):
        at_n = pl.ds(1024, 128) if not wide else pl.ds(pl.multiple_of(n * 256, 256), 256)
        value = dot3(xt_high[...], xt_low[...], z_high[:, at_n], z_low[:, at_n], 0)
        lower = lane(NB) < SIDE
        if wide:
            turned = jnp.concatenate(
                [jnp.where(lower, half_turn(value[:, h * 128:h * 128 + 128]), 0.0) for h in range(2)], axis=1)
        else:
            turned = jnp.where(lower, 0.0, half_turn(value))
        for part, shift in ((value, 0), (turned, SIDE)):
            high, low = split(part)
            for k in range(8):
                q_high[k * 128 + shift:k * 128 + shift + SIDE, at_n] = high[k * SIDE:(k + 1) * SIDE]
                q_low[k * 128 + shift:k * 128 + shift + SIDE, at_n] = low[k * SIDE:(k + 1) * SIDE]

    def left_task(g, n):
        rows = pl.ds(pl.multiple_of(g * 256, 256), 256)

        @pl.when(n == 0)
        def _():
            for h in range(2):
                a_high[h * 128:h * 128 + 128, :], a_low[h * 128:h * 128 + 128, :] = split(
                    jnp.transpose(w_all[2 * g + h]))

        @pl.when(n < 4)
        def _():
            at_n = pl.ds(pl.multiple_of(n * 256, 256), 256)
            value = dot3(a_high[...], a_low[...], q_high[:, at_n], q_low[:, at_n], 0)
            left_high[rows, at_n], left_low[rows, at_n] = split(value)

        @pl.when(n == 4)
        def _():
            value = dot3(a_high[...], a_low[...], q_high[:, 1024:1152], q_low[:, 1024:1152], 0)
            turned = jnp.transpose(value)
            low_ref[:, rows] = turned[:SIDE]
            red_ref[:, rows] = turned[SIDE:]

    def trail_task(block, i):
        if i == 0:
            for m in range(2):
                cols = pl.ds(m * 128, 128)
                b_high[:, cols], b_low[:, cols] = split(items[m, block])

        rows = pl.ds(i * 256, 256)
        value = dot3(left_high[rows, :], left_low[rows, :], b_high[...], b_low[...], 0)
        for m in range(2):
            cols = pl.ds(pl.multiple_of(m * ROWS + block * 128, 128), 128)
            trail[rows, cols] = trail[rows, cols] - value[:, m * 128:m * 128 + 128]

    def send_along(w):
        send(chunk(w, j), own_send.at[0], z_recv.at[0, w], up).start()
        send(chunk(w, j), own_send.at[1], z_recv.at[1, w], down).start()

    def tree(t):
        for m in range(2):
            q_copy, ready = unit_at(t + 2)

            @pl.when((depth[m] == 0) & ready)
            def _():
                at = unit(q_copy)
                pltpu.make_async_copy(
                    w_all.at[at[0], at[1], :], items.at[m, at[0], at[1], :], item_recv.at[m, q_copy]).start()

            q, here = unit_at(t - HOP * depth[m])

            @pl.when(here)
            def _():
                at = unit(q)
                part = items.at[m, at[0], at[1], :]
                arrived(part, item_recv.at[m, q])

                @pl.when(outs[m][0])
                def _():
                    send(part, item_send.at[m, 0], item_recv.at[m, q], plane[0]).start()
                    send(part, item_send.at[m, 1], item_recv.at[m, q], plane[1]).start()

                for d in (2, 3):
                    @pl.when(outs[m][d])
                    def _():
                        send(part, item_send.at[m, d], item_recv.at[m, q], plane[d]).start()

    def near(w):
        arrived(chunk(w, z_down), z_recv.at[0, w])
        arrived(chunk(w, z_up), z_recv.at[1, w])

        @pl.when(c == 0)
        def _():
            send(chunk(w, z_down), own_send.at[2], far_recv.at[w], up).start()

        @pl.when(c == 1)
        def _():
            send(chunk(w, z_up), own_send.at[2], far_recv.at[w], down).start()

        pl.when(w + W_OPEN < NW)(lambda: send_along(w + W_OPEN))
        send(chunk(w, z_down), sib_send.at[1], sib_recv.at[w], sib).start()
        send(chunk(w, z_up), sib_send.at[1], sib_recv.at[w], sib).start()

    def exchange(t):
        third = t % 3

        @pl.when((third == W_STEP % 3) & (t >= W_STEP) & (t < W_STEP + 3 * NW))
        def _():
            near((t - W_STEP) // 3)

        @pl.when(third == W_FAR % 3)
        def _():
            @pl.when((t >= W_FAR) & (t < W_FAR + 3 * NW))
            def _():
                w = (t - W_FAR) // 3
                arrived(chunk(w, z_far), far_recv.at[w])
                send(chunk(w, z_far), sib_send.at[1], sib_recv.at[w], sib).start()

            @pl.when((t >= W_DONE) & (t < W_DONE + 3 * NW))
            def _():
                w = (t - W_DONE) // 3
                arrived(w_all.at[w, pl.ds(0, 384), :], sib_recv.at[w])

    def matrices_near():
        first, second = xh_all.at[slot(z_down), :], xh_all.at[slot(z_up), :]
        arrived(first, xz_recv.at[0])
        arrived(second, xz_recv.at[1])

        @pl.when(c == 0)
        def _():
            send(first, x_send.at[2], xf_recv, up).start()

        @pl.when(c == 1)
        def _():
            send(second, x_send.at[2], xf_recv, down).start()

        send(first, sib_send.at[2], xs_recv, sib).start()
        send(second, sib_send.at[2], xs_recv, sib).start()

    def matrices_far():
        far = xh_all.at[slot(z_far), :]
        arrived(far, xf_recv)
        send(far, sib_send.at[2], xs_recv, sib).start()

    def matrices_all():
        arrived(xh_all.at[pl.ds(0, 512), :], xs_recv)
        prepare()

    def opening(t, carry):
        pl.when(t < W_OPEN)(lambda: send_along(t))

        @pl.when(t < NW)
        def _():
            send(chunk(t, j), sib_send.at[0], own_recv.at[t], sib).start()

        @pl.when((t >= 2) & (t < 2 + NW))
        def _():
            arrived(chunk(t - 2, j_sib), own_recv.at[t - 2])

        tree(t)
        return carry

    def small_step(t, carry):
        tree(t)
        exchange(t)
        pl.when(t == X_STEP)(matrices_near)
        pl.when(t == X_FAR)(matrices_far)

        @pl.when(t >= Q_STEP)
        def _():
            pl.when(t == Q_STEP)(matrices_all)
            pl.when(t == Q_STEP + 1)(half_product)
            pl.when(t == Q_STEP + 2)(diag_product)
            pl.when(t == Q_STEP + 3)(inner_product)

            @pl.when((t >= Q_STEP + 4) & (t < Q_STEP + 8))
            def _():
                weights(t - Q_STEP - 4, True)

            pl.when(t == Q_STEP + 8)(lambda: weights(0, False))

        return carry

    def left_step(t, carry):
        tree(t)
        exchange(t)
        left_task((t - Q_STEP - 9) // 5, (t - Q_STEP - 9) % 5)
        return carry

    def trail_steps(block, carry):
        for i in range(6):
            tree(U_READY + 6 * block + i)
            if i < 4:
                trail_task(block, i)
        return carry

    lax.fori_loop(0, 10, opening, 0)
    lax.fori_loop(10, Q_STEP + 9, small_step, 0)
    lax.fori_loop(Q_STEP + 9, U_READY, left_step, 0)
    pltpu.make_async_copy(t_hbm, trail, load_sem).wait()
    lax.fori_loop(0, 7, trail_steps, 0)
    for i in range(4):
        trail_task(7, i)

    own = w_all.at[:, slot(j), :]
    done = lambda ref, sem: send(ref, sem, own_recv.at[0], sib).wait_send()
    for i in range(3):
        done(own, own_send.at[i])
        done(own_x, x_send.at[i])
    done(own, sib_send.at[0])
    done(w_all.at[:, pl.ds(0, 384), :], sib_send.at[1])
    done(xh_all.at[pl.ds(0, 512), :], sib_send.at[2])
    for m in range(2):
        for d in range(4):
            @pl.when(outs[m][d])
            def _():
                done(items.at[m], item_send.at[m, d])


def on_device(s_panel, l_inv, h_diag, h_panel, h_trail):
    vmem = pl.BlockSpec(memory_space=pltpu.VMEM)
    hbm = pl.BlockSpec(memory_space=pltpu.HBM)
    dma = pltpu.SemaphoreType.DMA
    mats = [pltpu.VMEM((NB, NB), BF16)] * 8
    low, reduced, trailing = pl.pallas_call(
        kernel,
        out_shape=(
            pltpu.VMEM(s_panel.shape[::-1], F32),
            pltpu.VMEM(h_panel.shape[::-1], F32),
            pltpu.VMEM(h_trail.shape, F32),
        ),
        in_specs=[hbm] * 5,
        out_specs=(vmem, vmem, vmem),
        scratch_shapes=[
            pltpu.VMEM((NW, 1024, 128), F32), pltpu.VMEM((1024, NB), F32),
            pltpu.VMEM((2, NW, 1024, 128), F32),
            pltpu.VMEM((ROWS, 1024), BF16), pltpu.VMEM((ROWS, 1024), BF16),
            pltpu.VMEM((1024, 1152), BF16), pltpu.VMEM((1024, 1152), BF16),
            *mats,
            pltpu.VMEM((NB, NB), F32), pltpu.VMEM((NB, 1152), BF16), pltpu.VMEM((NB, 1152), BF16),
            *[pltpu.VMEM((256, 1024), BF16)] * 2, *[pltpu.VMEM((1024, 256), BF16)] * 2,
            dma((NW,)), dma((2, NW)), dma((NW,)), dma((NW,)), dma((2, UNITS)),
            dma((2,)), dma, dma, dma((3,)), dma((3,)), dma((3,)), dma((2, 4)),
            dma((NW + 1, 2)), dma,
        ],
        compiler_params=pltpu.CompilerParams(
            collective_id=0, has_side_effects=True, vmem_limit_bytes=55 * 2**20),
        cost_estimate=pl.CostEstimate(flops=22 * 10**9, bytes_accessed=20 * 2**20, transcendentals=0),
    )(s_panel.T, l_inv.T, h_diag.T, h_panel.T, h_trail)
    return low.T, reduced.T, trailing


def solution(mesh):
    in_specs = (P("row", "col"), P(None, "col"), P(None, "col"), P("row", "col"), P("row", "col"))
    out_specs = (P("row", "col"), P("row", "col"), P("row", "col"))
    return jax.shard_map(
        on_device, mesh=mesh, in_specs=in_specs, out_specs=out_specs, check_vma=False
    )
```

```python
import functools

import jax
import jax.numpy as jnp
from jax import lax
from jax.experimental import pallas as pl
from jax.experimental.pallas import tpu as pltpu
from jax.sharding import PartitionSpec as P

MESH = pl.DeviceIdType.MESH
F32, BF16 = jnp.float32, jnp.bfloat16
ROWS, NB, SIDE = 1024, 512, 64
NW = ROWS // 128
UNITS = 32
HOP = 6
LEAD = 4
GAP = 4
W_STEP = 12
W_FAR, W_DONE = W_STEP + 5, W_STEP + 8
W_OPEN = 2
X_STEP, X_FAR = W_STEP - 1, W_STEP + 4
Q_STEP = W_DONE
U_READY = LEAD + GAP + 4 * HOP + 22


def split(value):
    high = value.astype(BF16)
    return high, (value - high.astype(F32)).astype(BF16)


def dot3(a_high, a_low, b_high, b_low, b_dim):
    dims = (((1,), (b_dim,)), ((), ()))
    one = lambda a, b: lax.dot_general(a, b, dims, preferred_element_type=F32)
    return one(a_high, b_high) + (one(a_high, b_low) + one(a_low, b_high))


def half_turn(tile):
    return pltpu.roll(tile, SIDE, 1)


def kernel(s_hbm, x_hbm, d_hbm, p_hbm, t_hbm, low_ref, red_ref, trail,
           w_all, xh_all, items, left_high, left_low, q_high, q_low,
           x_high, x_low, xt_high, xt_low, m_high, m_low, n_high, n_low,
           d_full, z_high, z_low, a_high, a_low, b_high, b_low,
           own_recv, z_recv, far_recv, sib_recv, item_recv,
           xz_recv, xf_recv, xs_recv, own_send, sib_send, x_send, item_send,
           fetch_sem, load_sem):
    r, j = lax.axis_index("row"), lax.axis_index("col")
    y, x, z, c = r // 4, r % 4, j // 2, j % 2
    z_up, z_down, z_far = ((z + 1) % 4) * 2 + c, ((z + 3) % 4) * 2 + c, ((z + 2) % 4) * 2 + c
    j_sib = z * 2 + 1 - c
    up, down, sib = (r, z_up), (r, z_down), (r, j_sib)
    plane = [
        (y * 4 + (x + 1) % 4, j), (y * 4 + (x + 3) % 4, j),
        (((y + 1) % 4) * 4 + x, j), (((y + 3) % 4) * 4 + x, j),
    ]
    barrier = pltpu.get_barrier_semaphore()
    for device in plane + [up, down, sib]:
        pl.semaphore_signal(barrier, inc=1, device_id=device, device_id_type=MESH)

    slot = lambda k: pl.ds(pl.multiple_of(k * 128, 128), 128)
    lane = lambda rows, width=128: lax.broadcasted_iota(jnp.int32, (rows, width), 1)
    fetches = []
    for h, (panel, matrix) in enumerate(((s_hbm, x_hbm), (p_hbm, d_hbm))):
        at_h = pl.ds(pl.multiple_of(j * 128 + h * SIDE, SIDE), SIDE)
        fetches.append(pltpu.make_async_copy(matrix, xh_all.at[at_h, :], fetch_sem.at[8, h]))
        for w in range(NW):
            fetches.append(pltpu.make_async_copy(
                panel.at[:, pl.ds(w * 128, 128)], w_all.at[w, at_h, :], fetch_sem.at[w, h]))
    for fetch in fetches:
        fetch.start()
    load = pltpu.make_async_copy(t_hbm, trail, load_sem)
    load.start()
    for fetch in fetches:
        fetch.wait()
    pl.semaphore_wait(barrier, 7)

    def send(ref, send_sem, recv_sem, device):
        return pltpu.make_async_remote_copy(
            src_ref=ref, dst_ref=ref, send_sem=send_sem, recv_sem=recv_sem,
            device_id=device, device_id_type=MESH)

    def arrived(ref, sem):
        send(ref, sib_send.at[0], sem, sib).wait_recv()

    def chunk(w, k):
        return w_all.at[w, slot(k), :]

    f = (y + 4 - z) % 4
    outs, depth = [], []
    for m in range(2):
        e = (x + 4 - (2 * c + m)) % 4
        at = lambda a, b, e=e: (e == a) & (f == b)
        to_x = at(0, 0) | at(1, 1) | at(3, 3) | at(1, 2)
        to_up = at(1, 0) | at(1, 1) | at(1, 2)
        to_down = at(3, 0) | at(3, 3) | at(3, 2) | at(2, 1)
        outs.append([to_x, to_x, to_up, to_down])
        third = at(0, 3) | at(2, 3) | at(0, 1) | at(3, 2) | at(2, 1) | at(1, 2)
        depth.append(jnp.where(at(0, 0), 0, jnp.where(
            at(1, 0) | at(3, 0), 1, jnp.where(at(1, 1) | at(3, 3), 2, jnp.where(third, 3, 4)))))

    def unit(q):
        late = q >= 8
        block = jnp.where(late, (q + 1) // 3 - 3, q)
        which = (q + 1) % 3
        level = jnp.where(late, jnp.where(which == 0, z + 3, jnp.where(which == 1, z + 1, z + 2)), z) % 4
        return block, pl.ds(pl.multiple_of(level * 256, 256), 256)

    def unit_at(t):
        early = t < LEAD + 16
        late = t >= LEAD + 16 + GAP
        return (t - LEAD - jnp.where(late, GAP, 0)) // 2, (t >= LEAD) & (early | (late & (t < LEAD + GAP + 2 * UNITS)))

    own_x = xh_all.at[slot(j), :]
    send(own_x, sib_send.at[2], xs_recv, sib).start()
    send(own_x, x_send.at[0], xz_recv.at[0], up).start()
    send(own_x, x_send.at[1], xz_recv.at[1], down).start()

    def prepare():
        lower = lane(NB) < SIDE
        for p in range(4):
            rows = pl.ds(p * 128, 128)
            pair = [xh_all[256 * p + 128 * h:256 * p + 128 * h + 128, :] for h in range(2)]
            xt = jnp.concatenate([tile[:SIDE] for tile in pair], axis=0)
            dt = jnp.concatenate([tile[SIDE:] for tile in pair], axis=0)
            xt_high[rows, :], xt_low[rows, :] = split(xt)
            m_high[rows, :], m_low[rows, :] = split(dt)
            xv = jnp.transpose(xt)
            x_high[:, rows], x_low[:, rows] = split(xv)
            first, second = pl.ds(256 * p, 128), pl.ds(256 * p + 128, 128)
            z_high[:, first], z_low[:, first] = split(jnp.where(lower, 0.0, half_turn(xv)))
            z_high[:, second], z_low[:, second] = split(jnp.where(lower, 0.0, xv))

    def half_product():
        value = dot3(x_high[...], x_low[...], m_high[...], m_low[...], 1)
        n_high[...], n_low[...] = split(value)

    def diag_product():
        value = dot3(n_high[...], n_low[...], xt_high[...], xt_low[...], 0)
        d_full[...] = value
        m_high[...], m_low[...] = split(value)

    def inner_product():
        value = dot3(m_high[...], m_low[...], x_high[...], x_low[...], 0)
        lower = lane(NB) < SIDE
        for p in range(4):
            tile = value[:, 128 * p:128 * p + 128]
            for h in range(2):
                at_h = pl.ds(256 * p + 128 * h, 128)
                part = jnp.where(lower, -(tile if h == 0 else half_turn(tile)), 0.0)
                high, low = split(part)
                z_high[:, at_h] = jnp.where(lower, high, z_high[:, at_h])
                z_low[:, at_h] = jnp.where(lower, low, z_low[:, at_h])
        mine = d_full[:, pl.ds(pl.multiple_of(z * 128, 128), 128)]
        mine = jnp.where(c == 0, half_turn(mine), mine)
        row_id = lax.broadcasted_iota(jnp.int32, (NB, 128), 0)
        pick = jnp.where(row_id == lane(NB) + SIDE * j, 1.0, 0.0)
        z_high[:, 1024:1152], z_low[:, 1024:1152] = split(jnp.where(lower, pick, -mine))

    def weights(n, wide):
        at_n = pl.ds(1024, 128) if not wide else pl.ds(pl.multiple_of(n * 256, 256), 256)
        value = dot3(xt_high[...], xt_low[...], z_high[:, at_n], z_low[:, at_n], 0)
        lower = lane(NB) < SIDE
        if wide:
            turned = jnp.concatenate(
                [jnp.where(lower, half_turn(value[:, h * 128:h * 128 + 128]), 0.0) for h in range(2)], axis=1)
        else:
            turned = jnp.where(lower, 0.0, half_turn(value))
        for part, shift in ((value, 0), (turned, SIDE)):
            high, low = split(part)
            for k in range(8):
                q_high[k * 128 + shift:k * 128 + shift + SIDE, at_n] = high[k * SIDE:(k + 1) * SIDE]
                q_low[k * 128 + shift:k * 128 + shift + SIDE, at_n] = low[k * SIDE:(k + 1) * SIDE]

    def left_task(g, n):
        rows = pl.ds(pl.multiple_of(g * 512, 512), 512)

        @pl.when(n == 0)
        def _():
            for h in range(4):
                a_high[h * 128:h * 128 + 128, :], a_low[h * 128:h * 128 + 128, :] = split(
                    jnp.transpose(w_all[4 * g + h]))

        @pl.when(n < 4)
        def _():
            at_n = pl.ds(pl.multiple_of(n * 256, 256), 256)
            value = dot3(a_high[...], a_low[...], q_high[:, at_n], q_low[:, at_n], 0)
            left_high[rows, at_n], left_low[rows, at_n] = split(value)

        @pl.when(n == 4)
        def _():
            value = dot3(a_high[...], a_low[...], q_high[:, 1024:1152], q_low[:, 1024:1152], 0)
            turned = jnp.transpose(value)
            low_ref[:, rows] = turned[:SIDE]
            red_ref[:, rows] = turned[SIDE:]

    def trail_task(block, i):
        if i == 0:
            for m in range(2):
                cols = pl.ds(m * 128, 128)
                b_high[:, cols], b_low[:, cols] = split(items[m, block])

        rows = pl.ds(i * 1024, 1024)
        value = dot3(left_high[rows, :], left_low[rows, :], b_high[...], b_low[...], 0)
        for m in range(2):
            cols = pl.ds(pl.multiple_of(m * ROWS + block * 128, 128), 128)
            trail[rows, cols] = trail[rows, cols] - value[:, m * 128:m * 128 + 128]

    def send_along(w):
        send(chunk(w, j), own_send.at[0], z_recv.at[0, w], up).start()
        send(chunk(w, j), own_send.at[1], z_recv.at[1, w], down).start()

    def tree(t):
        m = t % 2
        mine = lambda pair: jnp.where(m == 0, pair[0].astype(jnp.int32), pair[1].astype(jnp.int32))
        level = mine(depth)
        q_copy, ready = unit_at(t + 2 - m)

        @pl.when((level == 0) & ready)
        def _():
            at = unit(q_copy)
            pltpu.make_async_copy(
                w_all.at[at[0], at[1], :], items.at[m, at[0], at[1], :], item_recv.at[m, q_copy]).start()

        q, here = unit_at(t - m - HOP * level)

        @pl.when(here)
        def _():
            at = unit(q)
            part = items.at[m, at[0], at[1], :]
            arrived(part, item_recv.at[m, q])

            @pl.when(mine([outs[0][0], outs[1][0]]) == 1)
            def _():
                send(part, item_send.at[m, 0], item_recv.at[m, q], plane[0]).start()
                send(part, item_send.at[m, 1], item_recv.at[m, q], plane[1]).start()

            for d in (2, 3):
                @pl.when(mine([outs[0][d], outs[1][d]]) == 1)
                def _():
                    send(part, item_send.at[m, d], item_recv.at[m, q], plane[d]).start()

    def near(w):
        arrived(chunk(w, z_down), z_recv.at[0, w])
        arrived(chunk(w, z_up), z_recv.at[1, w])

        @pl.when(c == 0)
        def _():
            send(chunk(w, z_down), own_send.at[2], far_recv.at[w], up).start()

        @pl.when(c == 1)
        def _():
            send(chunk(w, z_up), own_send.at[2], far_recv.at[w], down).start()

        pl.when(w + W_OPEN < NW)(lambda: send_along(w + W_OPEN))
        send(chunk(w, z_down), sib_send.at[1], sib_recv.at[w], sib).start()
        send(chunk(w, z_up), sib_send.at[1], sib_recv.at[w], sib).start()

    def exchange(t):
        third = t % 3

        @pl.when((third == W_STEP % 3) & (t >= W_STEP) & (t < W_STEP + 3 * NW))
        def _():
            near((t - W_STEP) // 3)

        @pl.when(third == W_FAR % 3)
        def _():
            @pl.when((t >= W_FAR) & (t < W_FAR + 3 * NW))
            def _():
                w = (t - W_FAR) // 3
                arrived(chunk(w, z_far), far_recv.at[w])
                send(chunk(w, z_far), sib_send.at[1], sib_recv.at[w], sib).start()

            @pl.when((t >= W_DONE) & (t < W_DONE + 3 * NW))
            def _():
                w = (t - W_DONE) // 3
                arrived(w_all.at[w, pl.ds(0, 384), :], sib_recv.at[w])

    def matrices_near():
        first, second = xh_all.at[slot(z_down), :], xh_all.at[slot(z_up), :]
        arrived(first, xz_recv.at[0])
        arrived(second, xz_recv.at[1])

        @pl.when(c == 0)
        def _():
            send(first, x_send.at[2], xf_recv, up).start()

        @pl.when(c == 1)
        def _():
            send(second, x_send.at[2], xf_recv, down).start()

        send(first, sib_send.at[2], xs_recv, sib).start()
        send(second, sib_send.at[2], xs_recv, sib).start()

    def matrices_far():
        far = xh_all.at[slot(z_far), :]
        arrived(far, xf_recv)
        send(far, sib_send.at[2], xs_recv, sib).start()

    def matrices_all():
        arrived(xh_all.at[pl.ds(0, 512), :], xs_recv)
        prepare()

    def opening(t, carry):
        pl.when(t < W_OPEN)(lambda: send_along(t))

        @pl.when(t < NW)
        def _():
            send(chunk(t, j), sib_send.at[0], own_recv.at[t], sib).start()

        @pl.when((t >= 2) & (t < 2 + NW))
        def _():
            arrived(chunk(t - 2, j_sib), own_recv.at[t - 2])

        tree(t)
        return carry

    def small_step(t, carry):
        tree(t)
        exchange(t)
        pl.when(t == X_STEP)(matrices_near)
        pl.when(t == X_FAR)(matrices_far)

        @pl.when(t >= Q_STEP)
        def _():
            pl.when(t == Q_STEP)(matrices_all)
            pl.when(t == Q_STEP + 1)(half_product)
            pl.when(t == Q_STEP + 2)(diag_product)
            pl.when(t == Q_STEP + 3)(inner_product)

            @pl.when((t >= Q_STEP + 4) & (t < Q_STEP + 8))
            def _():
                weights(t - Q_STEP - 4, True)

            pl.when(t == Q_STEP + 8)(lambda: weights(0, False))

        return carry

    def left_step(t, carry):
        tree(t)
        exchange(t)

        past = t - Q_STEP - 10

        @pl.when((past >= 0) & (past % 2 == 0) & (past % 12 < 10))
        def _():
            left_task(past // 12, past % 12 // 2)

        return carry

    def trail_steps(block, carry):
        for i in range(6):
            tree(U_READY + 6 * block + i)
            if i == 0:
                trail_task(block, i)
        return carry

    lax.fori_loop(0, 10, opening, 0)
    lax.fori_loop(10, Q_STEP + 9, small_step, 0)
    lax.fori_loop(Q_STEP + 9, U_READY, left_step, 0)
    pltpu.make_async_copy(t_hbm, trail, load_sem).wait()
    lax.fori_loop(0, 7, trail_steps, 0)
    for i in range(1):
        trail_task(7, i)

    own = w_all.at[:, slot(j), :]
    done = lambda ref, sem: send(ref, sem, own_recv.at[0], sib).wait_send()
    for i in range(3):
        done(own, own_send.at[i])
        done(own_x, x_send.at[i])
    done(own, sib_send.at[0])
    done(w_all.at[:, pl.ds(0, 384), :], sib_send.at[1])
    done(xh_all.at[pl.ds(0, 512), :], sib_send.at[2])
    for m in range(2):
        for d in range(4):
            @pl.when(outs[m][d])
            def _():
                done(items.at[m], item_send.at[m, d])


def on_device(s_panel, l_inv, h_diag, h_panel, h_trail):
    vmem = pl.BlockSpec(memory_space=pltpu.VMEM)
    hbm = pl.BlockSpec(memory_space=pltpu.HBM)
    dma = pltpu.SemaphoreType.DMA
    mats = [pltpu.VMEM((NB, NB), BF16)] * 8
    low, reduced, trailing = pl.pallas_call(
        kernel,
        out_shape=(
            pltpu.VMEM(s_panel.shape[::-1], F32),
            pltpu.VMEM(h_panel.shape[::-1], F32),
            pltpu.VMEM(h_trail.shape, F32),
        ),
        in_specs=[hbm] * 5,
        out_specs=(vmem, vmem, vmem),
        scratch_shapes=[
            pltpu.VMEM((NW, 1024, 128), F32), pltpu.VMEM((1024, NB), F32),
            pltpu.VMEM((2, NW, 1024, 128), F32),
            pltpu.VMEM((ROWS, 1024), BF16), pltpu.VMEM((ROWS, 1024), BF16),
            pltpu.VMEM((1024, 1152), BF16), pltpu.VMEM((1024, 1152), BF16),
            *mats,
            pltpu.VMEM((NB, NB), F32), pltpu.VMEM((NB, 1152), BF16), pltpu.VMEM((NB, 1152), BF16),
            *[pltpu.VMEM((512, 1024), BF16)] * 2, *[pltpu.VMEM((1024, 256), BF16)] * 2,
            dma((NW,)), dma((2, NW)), dma((NW,)), dma((NW,)), dma((2, UNITS)),
            dma((2,)), dma, dma, dma((3,)), dma((3,)), dma((3,)), dma((2, 4)),
            dma((NW + 1, 2)), dma,
        ],
        compiler_params=pltpu.CompilerParams(
            collective_id=0, has_side_effects=True, vmem_limit_bytes=55 * 2**20),
        cost_estimate=pl.CostEstimate(flops=22 * 10**9, bytes_accessed=20 * 2**20, transcendentals=0),
    )(s_panel.T, l_inv.T, h_diag.T, h_panel.T, h_trail)
    return low.T, reduced.T, trailing


def solution(mesh):
    in_specs = (P("row", "col"), P(None, "col"), P(None, "col"), P("row", "col"), P("row", "col"))
    out_specs = (P("row", "col"), P("row", "col"), P("row", "col"))
    return jax.shard_map(
        on_device, mesh=mesh, in_specs=in_specs, out_specs=out_specs, check_vma=False
    )
```

```python
import functools

import jax
import jax.numpy as jnp
from jax import lax
from jax.experimental import pallas as pl
from jax.experimental.pallas import tpu as pltpu
from jax.sharding import PartitionSpec as P

MESH = pl.DeviceIdType.MESH
F32, BF16 = jnp.float32, jnp.bfloat16
ROWS, NB, SIDE = 1024, 512, 64
NW = ROWS // 128
UNITS = 32
HOP = 6
LEAD = 4
GAP = 4
W_STEP = 12
W_FAR, W_DONE = W_STEP + 5, W_STEP + 8
W_OPEN = 2
X_STEP, X_FAR = W_STEP - 1, W_STEP + 4
Q_STEP = W_DONE
U_READY = LEAD + GAP + 4 * HOP + 22
LEFT_STEP = Q_STEP + 18
TRAIL_STEP = U_READY + 7


def split(value):
    high = value.astype(BF16)
    return high, (value - high.astype(F32)).astype(BF16)


def dot3(a_high, a_low, b_high, b_low, b_dim):
    dims = (((1,), (b_dim,)), ((), ()))
    one = lambda a, b: lax.dot_general(a, b, dims, preferred_element_type=F32)
    return one(a_high, b_high) + (one(a_high, b_low) + one(a_low, b_high))


def half_turn(tile):
    return pltpu.roll(tile, SIDE, 1)


def kernel(s_hbm, x_hbm, d_hbm, p_hbm, t_hbm, low_ref, red_ref, trail,
           w_all, xh_all, items, left_high, left_low, q_high, q_low,
           x_high, x_low, xt_high, xt_low, m_high, m_low, n_high, n_low,
           d_full, z_high, z_low, a_high, a_low, b_high, b_low,
           own_recv, z_recv, far_recv, sib_recv, item_recv,
           xz_recv, xf_recv, xs_recv, own_send, sib_send, x_send, item_send,
           fetch_sem, load_sem):
    r, j = lax.axis_index("row"), lax.axis_index("col")
    y, x, z, c = r // 4, r % 4, j // 2, j % 2
    z_up, z_down, z_far = ((z + 1) % 4) * 2 + c, ((z + 3) % 4) * 2 + c, ((z + 2) % 4) * 2 + c
    j_sib = z * 2 + 1 - c
    up, down, sib = (r, z_up), (r, z_down), (r, j_sib)
    plane = [
        (y * 4 + (x + 1) % 4, j), (y * 4 + (x + 3) % 4, j),
        (((y + 1) % 4) * 4 + x, j), (((y + 3) % 4) * 4 + x, j),
    ]
    barrier = pltpu.get_barrier_semaphore()
    for device in plane + [up, down, sib]:
        pl.semaphore_signal(barrier, inc=1, device_id=device, device_id_type=MESH)

    slot = lambda k: pl.ds(pl.multiple_of(k * 128, 128), 128)
    lane = lambda rows, width=128: lax.broadcasted_iota(jnp.int32, (rows, width), 1)
    fetches = []
    for h, (panel, matrix) in enumerate(((s_hbm, x_hbm), (p_hbm, d_hbm))):
        at_h = pl.ds(pl.multiple_of(j * 128 + h * SIDE, SIDE), SIDE)
        fetches.append(pltpu.make_async_copy(matrix, xh_all.at[at_h, :], fetch_sem.at[8, h]))
        for w in range(NW):
            fetches.append(pltpu.make_async_copy(
                panel.at[:, pl.ds(w * 128, 128)], w_all.at[w, at_h, :], fetch_sem.at[w, h]))
    for fetch in fetches:
        fetch.start()
    load = pltpu.make_async_copy(t_hbm, trail, load_sem)
    load.start()
    for fetch in fetches:
        fetch.wait()
    pl.semaphore_wait(barrier, 7)

    def send(ref, send_sem, recv_sem, device):
        return pltpu.make_async_remote_copy(
            src_ref=ref, dst_ref=ref, send_sem=send_sem, recv_sem=recv_sem,
            device_id=device, device_id_type=MESH)

    def arrived(ref, sem):
        send(ref, sib_send.at[0], sem, sib).wait_recv()

    def chunk(w, k):
        return w_all.at[w, slot(k), :]

    f = (y + 4 - z) % 4
    outs, depth = [], []
    for m in range(2):
        e = (x + 4 - (2 * c + m)) % 4
        at = lambda a, b, e=e: (e == a) & (f == b)
        to_x = at(0, 0) | at(1, 1) | at(3, 3) | at(1, 2)
        to_up = at(1, 0) | at(1, 1) | at(1, 2)
        to_down = at(3, 0) | at(3, 3) | at(3, 2) | at(2, 1)
        outs.append([to_x, to_x, to_up, to_down])
        third = at(0, 3) | at(2, 3) | at(0, 1) | at(3, 2) | at(2, 1) | at(1, 2)
        depth.append(jnp.where(at(0, 0), 0, jnp.where(
            at(1, 0) | at(3, 0), 1, jnp.where(at(1, 1) | at(3, 3), 2, jnp.where(third, 3, 4)))))

    def unit(q):
        late = q >= 8
        block = jnp.where(late, (q + 1) // 3 - 3, q)
        which = (q + 1) % 3
        level = jnp.where(late, jnp.where(which == 0, z + 3, jnp.where(which == 1, z + 1, z + 2)), z) % 4
        return block, pl.ds(pl.multiple_of(level * 256, 256), 256)

    def unit_at(t):
        early = t < LEAD + 16
        late = t >= LEAD + 16 + GAP
        return (t - LEAD - jnp.where(late, GAP, 0)) // 2, (t >= LEAD) & (early | (late & (t < LEAD + GAP + 2 * UNITS)))

    own_x = xh_all.at[slot(j), :]
    send(own_x, sib_send.at[2], xs_recv, sib).start()
    send(own_x, x_send.at[0], xz_recv.at[0], up).start()
    send(own_x, x_send.at[1], xz_recv.at[1], down).start()

    def prepare():
        lower = lane(NB) < SIDE
        for p in range(4):
            rows = pl.ds(p * 128, 128)
            pair = [xh_all[256 * p + 128 * h:256 * p + 128 * h + 128, :] for h in range(2)]
            xt = jnp.concatenate([tile[:SIDE] for tile in pair], axis=0)
            dt = jnp.concatenate([tile[SIDE:] for tile in pair], axis=0)
            xt_high[rows, :], xt_low[rows, :] = split(xt)
            m_high[rows, :], m_low[rows, :] = split(dt)
            xv = jnp.transpose(xt)
            x_high[:, rows], x_low[:, rows] = split(xv)
            first, second = pl.ds(256 * p, 128), pl.ds(256 * p + 128, 128)
            z_high[:, first], z_low[:, first] = split(jnp.where(lower, 0.0, half_turn(xv)))
            z_high[:, second], z_low[:, second] = split(jnp.where(lower, 0.0, xv))

    def half_product():
        value = dot3(x_high[...], x_low[...], m_high[...], m_low[...], 1)
        n_high[...], n_low[...] = split(value)

    def diag_product():
        value = dot3(n_high[...], n_low[...], xt_high[...], xt_low[...], 0)
        d_full[...] = value
        m_high[...], m_low[...] = split(value)

    def inner_product():
        value = dot3(m_high[...], m_low[...], x_high[...], x_low[...], 0)
        lower = lane(NB) < SIDE
        for p in range(4):
            tile = value[:, 128 * p:128 * p + 128]
            for h in range(2):
                at_h = pl.ds(256 * p + 128 * h, 128)
                part = jnp.where(lower, -(tile if h == 0 else half_turn(tile)), 0.0)
                high, low = split(part)
                z_high[:, at_h] = jnp.where(lower, high, z_high[:, at_h])
                z_low[:, at_h] = jnp.where(lower, low, z_low[:, at_h])
        mine = d_full[:, pl.ds(pl.multiple_of(z * 128, 128), 128)]
        mine = jnp.where(c == 0, half_turn(mine), mine)
        row_id = lax.broadcasted_iota(jnp.int32, (NB, 128), 0)
        pick = jnp.where(row_id == lane(NB) + SIDE * j, 1.0, 0.0)
        z_high[:, 1024:1152], z_low[:, 1024:1152] = split(jnp.where(lower, pick, -mine))

    def weights(n, wide):
        at_n = pl.ds(1024, 128) if not wide else pl.ds(pl.multiple_of(n * 256, 256), 256)
        value = dot3(xt_high[...], xt_low[...], z_high[:, at_n], z_low[:, at_n], 0)
        lower = lane(NB) < SIDE
        if wide:
            turned = jnp.concatenate(
                [jnp.where(lower, half_turn(value[:, h * 128:h * 128 + 128]), 0.0) for h in range(2)], axis=1)
        else:
            turned = jnp.where(lower, 0.0, half_turn(value))
        for part, shift in ((value, 0), (turned, SIDE)):
            high, low = split(part)
            for k in range(8):
                q_high[k * 128 + shift:k * 128 + shift + SIDE, at_n] = high[k * SIDE:(k + 1) * SIDE]
                q_low[k * 128 + shift:k * 128 + shift + SIDE, at_n] = low[k * SIDE:(k + 1) * SIDE]

    def left_task(g, n):
        rows = pl.ds(pl.multiple_of(g * 512, 512), 512)

        @pl.when(n == 0)
        def _():
            for h in range(4):
                a_high[h * 128:h * 128 + 128, :], a_low[h * 128:h * 128 + 128, :] = split(
                    jnp.transpose(w_all[4 * g + h]))

        @pl.when(n < 4)
        def _():
            at_n = pl.ds(pl.multiple_of(n * 256, 256), 256)
            value = dot3(a_high[...], a_low[...], q_high[:, at_n], q_low[:, at_n], 0)
            left_high[rows, at_n], left_low[rows, at_n] = split(value)

        @pl.when(n == 4)
        def _():
            value = dot3(a_high[...], a_low[...], q_high[:, 1024:1152], q_low[:, 1024:1152], 0)
            turned = jnp.transpose(value)
            low_ref[:, rows] = turned[:SIDE]
            red_ref[:, rows] = turned[SIDE:]

    def trail_task(block, i):
        if i == 0:
            for m in range(2):
                cols = pl.ds(m * 128, 128)
                b_high[:, cols], b_low[:, cols] = split(items[m, block])

        rows = pl.ds(i * 1024, 1024)
        value = dot3(left_high[rows, :], left_low[rows, :], b_high[...], b_low[...], 0)
        for m in range(2):
            cols = pl.ds(pl.multiple_of(m * ROWS + block * 128, 128), 128)
            trail[rows, cols] = trail[rows, cols] - value[:, m * 128:m * 128 + 128]

    def send_along(w):
        send(chunk(w, j), own_send.at[0], z_recv.at[0, w], up).start()
        send(chunk(w, j), own_send.at[1], z_recv.at[1, w], down).start()

    def tree(t):
        m = t % 2
        mine = lambda pair: jnp.where(m == 0, pair[0].astype(jnp.int32), pair[1].astype(jnp.int32))
        level = mine(depth)
        q_copy, ready = unit_at(t + 2 - m)

        @pl.when((level == 0) & ready)
        def _():
            at = unit(q_copy)
            pltpu.make_async_copy(
                w_all.at[at[0], at[1], :], items.at[m, at[0], at[1], :], item_recv.at[m, q_copy]).start()

        q, here = unit_at(t - m - HOP * level)

        @pl.when(here)
        def _():
            at = unit(q)
            part = items.at[m, at[0], at[1], :]
            arrived(part, item_recv.at[m, q])

            @pl.when(mine([outs[0][0], outs[1][0]]) == 1)
            def _():
                send(part, item_send.at[m, 0], item_recv.at[m, q], plane[0]).start()
                send(part, item_send.at[m, 1], item_recv.at[m, q], plane[1]).start()

            for d in (2, 3):
                @pl.when(mine([outs[0][d], outs[1][d]]) == 1)
                def _():
                    send(part, item_send.at[m, d], item_recv.at[m, q], plane[d]).start()

    def near(w):
        arrived(chunk(w, z_down), z_recv.at[0, w])
        arrived(chunk(w, z_up), z_recv.at[1, w])

        @pl.when(c == 0)
        def _():
            send(chunk(w, z_down), own_send.at[2], far_recv.at[w], up).start()

        @pl.when(c == 1)
        def _():
            send(chunk(w, z_up), own_send.at[2], far_recv.at[w], down).start()

        pl.when(w + W_OPEN < NW)(lambda: send_along(w + W_OPEN))
        send(chunk(w, z_down), sib_send.at[1], sib_recv.at[w], sib).start()
        send(chunk(w, z_up), sib_send.at[1], sib_recv.at[w], sib).start()

    def exchange(t):
        third = t % 3

        @pl.when((third == W_STEP % 3) & (t >= W_STEP) & (t < W_STEP + 3 * NW))
        def _():
            near((t - W_STEP) // 3)

        @pl.when(third == W_FAR % 3)
        def _():
            @pl.when((t >= W_FAR) & (t < W_FAR + 3 * NW))
            def _():
                w = (t - W_FAR) // 3
                arrived(chunk(w, z_far), far_recv.at[w])
                send(chunk(w, z_far), sib_send.at[1], sib_recv.at[w], sib).start()

            @pl.when((t >= W_DONE) & (t < W_DONE + 3 * NW))
            def _():
                w = (t - W_DONE) // 3
                arrived(w_all.at[w, pl.ds(0, 384), :], sib_recv.at[w])

    def matrices_near():
        first, second = xh_all.at[slot(z_down), :], xh_all.at[slot(z_up), :]
        arrived(first, xz_recv.at[0])
        arrived(second, xz_recv.at[1])

        @pl.when(c == 0)
        def _():
            send(first, x_send.at[2], xf_recv, up).start()

        @pl.when(c == 1)
        def _():
            send(second, x_send.at[2], xf_recv, down).start()

        send(first, sib_send.at[2], xs_recv, sib).start()
        send(second, sib_send.at[2], xs_recv, sib).start()

    def matrices_far():
        far = xh_all.at[slot(z_far), :]
        arrived(far, xf_recv)
        send(far, sib_send.at[2], xs_recv, sib).start()

    def matrices_all():
        arrived(xh_all.at[pl.ds(0, 512), :], xs_recv)
        prepare()

    def opening(t, carry):
        pl.when(t < W_OPEN)(lambda: send_along(t))

        @pl.when(t < NW)
        def _():
            send(chunk(t, j), sib_send.at[0], own_recv.at[t], sib).start()

        @pl.when((t >= 2) & (t < 2 + NW))
        def _():
            arrived(chunk(t - 2, j_sib), own_recv.at[t - 2])

        tree(t)
        return carry

    def small_step(t, carry):
        tree(t)
        exchange(t)
        pl.when(t == X_STEP)(matrices_near)
        pl.when(t == X_FAR)(matrices_far)

        task, rest = (t - Q_STEP) // 2, (t - Q_STEP) % 2

        @pl.when((t >= Q_STEP) & (rest == 0))
        def _():
            pl.when(task == 0)(matrices_all)
            pl.when(task == 1)(half_product)
            pl.when(task == 2)(diag_product)
            pl.when(task == 3)(inner_product)

            @pl.when((task >= 4) & (task < 8))
            def _():
                weights(task - 4, True)

            pl.when(task == 8)(lambda: weights(0, False))

        return carry

    def left_step(t, carry):
        tree(t)
        exchange(t)

        past = t - LEFT_STEP
        task = past // 5 * 2 + past % 5 // 2

        @pl.when((past % 5 == 0) | (past % 5 == 2))
        def _():
            left_task(task // 5, task % 5)

        return carry

    def last_block(k, carry):
        at_k = pl.ds(pl.multiple_of((z + 3 + k) % 4 * 256, 256), 256)
        for m in range(2):
            cols = pl.ds(m * 128, 128)
            b_high[:256, cols], b_low[:256, cols] = split(items[m, NW - 1, at_k, :])
        value = dot3(left_high[:, at_k], left_low[:, at_k], b_high[:256, :], b_low[:256, :], 0)
        for m in range(2):
            cols = pl.ds((m + 1) * ROWS - 128, 128)
            trail[:, cols] = trail[:, cols] - value[:, m * 128:m * 128 + 128]
        return carry

    def most_of_last():
        lax.fori_loop(0, 3, last_block, 0)

    def trail_steps(block, carry):
        for i in range(5):
            tree(TRAIL_STEP + 5 * block + i)
            if i == 0:
                trail_task(block, i)
            if i == 3:
                pl.when(block == 6)(most_of_last)
        return carry

    lax.fori_loop(0, 10, opening, 0)
    lax.fori_loop(10, LEFT_STEP, small_step, 0)
    lax.fori_loop(LEFT_STEP, TRAIL_STEP, left_step, 0)
    pltpu.make_async_copy(t_hbm, trail, load_sem).wait()
    lax.fori_loop(0, 7, trail_steps, 0)
    last_block(3, None)

    own = w_all.at[:, slot(j), :]
    done = lambda ref, sem: send(ref, sem, own_recv.at[0], sib).wait_send()
    for i in range(3):
        done(own, own_send.at[i])
        done(own_x, x_send.at[i])
    done(own, sib_send.at[0])
    done(w_all.at[:, pl.ds(0, 384), :], sib_send.at[1])
    done(xh_all.at[pl.ds(0, 512), :], sib_send.at[2])
    for m in range(2):
        for d in range(4):
            @pl.when(outs[m][d])
            def _():
                done(items.at[m], item_send.at[m, d])


def on_device(s_panel, l_inv, h_diag, h_panel, h_trail):
    vmem = pl.BlockSpec(memory_space=pltpu.VMEM)
    hbm = pl.BlockSpec(memory_space=pltpu.HBM)
    dma = pltpu.SemaphoreType.DMA
    mats = [pltpu.VMEM((NB, NB), BF16)] * 8
    low, reduced, trailing = pl.pallas_call(
        kernel,
        out_shape=(
            pltpu.VMEM(s_panel.shape[::-1], F32),
            pltpu.VMEM(h_panel.shape[::-1], F32),
            pltpu.VMEM(h_trail.shape, F32),
        ),
        in_specs=[hbm] * 5,
        out_specs=(vmem, vmem, vmem),
        scratch_shapes=[
            pltpu.VMEM((NW, 1024, 128), F32), pltpu.VMEM((1024, NB), F32),
            pltpu.VMEM((2, NW, 1024, 128), F32),
            pltpu.VMEM((ROWS, 1024), BF16), pltpu.VMEM((ROWS, 1024), BF16),
            pltpu.VMEM((1024, 1152), BF16), pltpu.VMEM((1024, 1152), BF16),
            *mats,
            pltpu.VMEM((NB, NB), F32), pltpu.VMEM((NB, 1152), BF16), pltpu.VMEM((NB, 1152), BF16),
            *[pltpu.VMEM((512, 1024), BF16)] * 2, *[pltpu.VMEM((1024, 256), BF16)] * 2,
            dma((NW,)), dma((2, NW)), dma((NW,)), dma((NW,)), dma((2, UNITS)),
            dma((2,)), dma, dma, dma((3,)), dma((3,)), dma((3,)), dma((2, 4)),
            dma((NW + 1, 2)), dma,
        ],
        compiler_params=pltpu.CompilerParams(
            collective_id=0, has_side_effects=True, vmem_limit_bytes=55 * 2**20),
        cost_estimate=pl.CostEstimate(flops=22 * 10**9, bytes_accessed=20 * 2**20, transcendentals=0),
    )(s_panel.T, l_inv.T, h_diag.T, h_panel.T, h_trail)
    return low.T, reduced.T, trailing


def solution(mesh):
    in_specs = (P("row", "col"), P(None, "col"), P(None, "col"), P("row", "col"), P("row", "col"))
    out_specs = (P("row", "col"), P("row", "col"), P("row", "col"))
    return jax.shard_map(
        on_device, mesh=mesh, in_specs=in_specs, out_specs=out_specs, check_vma=False
    )
```
